128 devices in a mesh: leaf: 32 (over y, z, core), sub: 4 (over x).
Axes of the slice: x: 4, y: 4, z: 4, core: 2. Of those that a mesh axis runs over, the one named last changes fastest.
Arguments:
- points: float32 [8192, 8, 128], P(('leaf', 'sub')), may hold values from -6 to 6
- probes: bfloat16 [8192, 32, 128], P(('leaf', 'sub')), may hold values from -6 to 6
- leaf_basis: bfloat16 [8192, 64, 128], P(('leaf', 'sub')), may hold values from -0.5 to 0.5
- mid_transfer: float32 [8192, 64, 64], P(('leaf', 'sub')), may hold values from -0.25 to 0.25
- top_transfer: float32 [1024, 64, 64], P(('leaf', 'sub')), may hold values from -0.25 to 0.25
- mid_skeleton: float32 [1024, 8, 64], P(('leaf', 'sub')), may hold values from -6 to 6
- top_skeleton: float32 [32, 8, 64], replicated, may hold values from -6 to 6
- near_list: int32 [8192, 8], P(('leaf', 'sub')), may hold values from -1 to 8191, as said below
- mid_list: int32 [1024, 6], P(('leaf', 'sub')), may hold values from -1 to 1023, as said below
- top_list: int32 [32, 6], P('leaf'), may hold values from -1 to 31, as said below
- inv_scale: float32 [8], replicated, may hold values from 0.15 to 0.5
- amplitude: float32 [1], replicated, may hold values from 0.03 to 0.1
- noise_var: float32 [1], replicated, may hold values from 0.2 to 1
Outputs:
- first_product: bfloat16 [8192, 32, 128], P(('leaf', 'sub'))
- second_product: bfloat16 [8192, 32, 128], P(('leaf', 'sub'))
The draws below stay inside these ranges and needn't reach their ends.
Inputs may be any that keep to these rules, and one draw needn't show every extreme that they name: `near_list`: entry 0 of row i is i; the other entries of a row are distinct leaves j != i with |j - i| <= 64, or -1. `mid_list`: the entries of a row m are distinct middle clusters j != m with |j - m| <= 8, or -1. `top_list`: the entries of a row t are distinct top clusters other than t, or -1.
All inputs are finite; a program needn't handle non-finite values.
Results may differ from the reference program's by a relative error of at most 0.0042.
Values may be sent and summed in bfloat16 or wider, within the bound.
A program may use at most 128 MiB of HBM per device.

```python
import math
import jax
import jax.numpy as jnp
from jax import lax

LEAF = 128
R = 64
FEAT = 8
PROBES = 32
MID = 8
NEAR = 8
MID_NEAR = 6
TOP_NEAR = 6
LEAF_DEV = 64
MID_DEV = 8
NLEAF = 8192
NMID = 1024
NTOP = 32


def pick_lists(key, rows, reach, count, keep_every):
    row_ids = jnp.arange(rows, dtype=jnp.int32)
    scores = jax.random.randint(key, (rows, 2 * reach), 0, 1048576)
    order = jnp.argsort(scores, axis=1, stable=True)[:, :count].astype(jnp.int32)
    offsets = jnp.where(order < reach, order - reach, order - reach + 1)
    targets = row_ids[:, None] + offsets
    keeping = jax.random.randint(jax.random.fold_in(key, 7), (rows, count), 0, 4) != 0
    keeping = keeping | (row_ids[:, None] % keep_every == 0)
    inside = (targets >= 0) & (targets < rows)
    return jnp.where(keeping & inside, targets, -1).astype(jnp.int32)


def draw_near_list(key, part):
    local_key = jax.random.fold_in(key, 101)
    others = pick_lists(local_key, NLEAF, LEAF_DEV, NEAR - 1, 5)
    selves = jnp.arange(NLEAF, dtype=jnp.int32)[:, None]
    return jnp.concatenate([selves, others], axis=1).astype(jnp.int32)


def draw_mid_list(key, part):
    local_key = jax.random.fold_in(key, 202)
    return pick_lists(local_key, NMID, MID_DEV, MID_NEAR, 3)


def draw_top_list(key, part):
    local_key = jax.random.fold_in(key, 303)
    row_ids = jnp.arange(NTOP, dtype=jnp.int32)
    scores = jax.random.randint(local_key, (NTOP, NTOP), 0, 1048576)
    scores = scores + (row_ids[:, None] == row_ids[None, :]).astype(jnp.int32) * 2097152
    order = jnp.argsort(scores, axis=1, stable=True)[:, :TOP_NEAR].astype(jnp.int32)
    keeping = jax.random.randint(jax.random.fold_in(local_key, 9), (NTOP, TOP_NEAR), 0, 4) != 0
    keeping = keeping | (row_ids[:, None] % 2 == 0)
    return jnp.where(keeping, order, -1).astype(jnp.int32)


def block_levels(rng, shape, pieces, low, largest):
    gain, own = 1.0, jax.random.fold_in(rng, 6)
    for dim, shards_of in pieces:
        steps = jnp.exp(jax.random.uniform(jax.random.fold_in(own, dim), (shards_of,), jnp.float32, low / len(pieces), largest / len(pieces)))
        gain = gain * jnp.repeat(steps, shape[dim] // shards_of).reshape([-1 if axis == dim else 1 for axis in range(len(shape))])
    return gain


def noise(rng, dims, width, most, split=(), kind=jnp.bfloat16):
    result = width * jax.random.normal(rng, dims, jnp.float32)
    if split:
        result = result * block_levels(rng, dims, split, -0.22, 0.18)
    return jnp.clip(result, -most, most).astype(kind)


def setup_inputs(seed: int = 0) -> dict:
    arg_keys = jax.random.split(jax.random.key(seed), 14)
    return {
        "points": noise(arg_keys[0], (NLEAF, FEAT, LEAF), 1.0, 6.0, ((0, 128),), jnp.float32),
        "probes": noise(arg_keys[1], (NLEAF, PROBES, LEAF), 1.0, 6.0, ((0, 128),)),
        "leaf_basis": noise(arg_keys[2], (NLEAF, R, LEAF), LEAF ** -0.5, 0.5, ((0, 128),)),
        "mid_transfer": noise(arg_keys[3], (NLEAF, R, R), (R * MID) ** -0.5, 0.25, ((0, 128),), jnp.float32),
        "top_transfer": noise(arg_keys[4], (NMID, R, R), (R * MID_DEV) ** -0.5, 0.25, ((0, 128),), jnp.float32),
        "mid_skeleton": noise(arg_keys[5], (NMID, FEAT, R), 1.0, 6.0, ((0, 128),), jnp.float32),
        "top_skeleton": noise(arg_keys[6], (NTOP, FEAT, R), 1.0, 6.0, (), jnp.float32),
        "near_list": draw_near_list(jax.random.fold_in(arg_keys[13], 71), 0),
        "mid_list": draw_mid_list(jax.random.fold_in(arg_keys[13], 71), 0),
        "top_list": draw_top_list(jax.random.fold_in(arg_keys[13], 71), 0),
        "inv_scale": jnp.clip(jnp.exp(jax.random.uniform(arg_keys[10], (FEAT,), jnp.float32, math.log(0.15), math.log(0.5))), 0.15, 0.5),
        "amplitude": jnp.clip(jnp.exp(jax.random.uniform(arg_keys[11], (1,), jnp.float32, math.log(0.03), math.log(0.1))), 0.03, 0.1),
        "noise_var": jnp.clip(jnp.exp(jax.random.uniform(arg_keys[12], (1,), jnp.float32, math.log(0.2), math.log(1.0))), 0.2, 1.0),
    }


def matern(left_side, right_side, inv_scale, amplitude):
    accumulated = None
    for feature in range(left_side.shape[-2]):
        difference = (left_side[..., feature, :, None] - right_side[..., feature, None, :]) * inv_scale[feature]
        if accumulated is None:
            accumulated = difference * difference
        else:
            accumulated = accumulated + difference * difference
    scaled = jnp.sqrt(3.0 * accumulated)
    return amplitude * (1.0 + scaled) * jnp.exp(-scaled)

def coupling(skeleton_own, skeleton_all, entries, inv_scale, amplitude):
    present = entries >= 0
    clipped = jnp.where(present, entries, 0)
    kernel_block = matern(skeleton_own[None], skeleton_all[clipped], inv_scale, amplitude)
    return kernel_block * present[:, None, None].astype(jnp.float32)

def near_part(points, vector, near_list, inv_scale, amplitude):

    def per_leaf(item):
        own_points, entries = item
        present = entries >= 0
        clipped = jnp.where(present, entries, 0)
        kernel_block = matern(own_points[None], points[clipped], inv_scale, amplitude)
        kernel_block = (kernel_block * present[:, None, None].astype(jnp.float32)).astype(jnp.bfloat16)
        gathered = vector[clipped]
        return jnp.einsum('knm,kpm->pn', kernel_block.astype(jnp.float32), gathered.astype(jnp.float32))
    return lax.map(per_leaf, (points, near_list))

def reference(points, probes, leaf_basis, mid_transfer, top_transfer, mid_skeleton, top_skeleton, near_list, mid_list, top_list, inv_scale, amplitude, noise_var):
    highest = lax.Precision.HIGHEST
    scale_amp = amplitude[0]
    mid_coupling = jax.vmap(lambda own, entries: coupling(own, mid_skeleton, entries, inv_scale, scale_amp))(mid_skeleton, mid_list)
    top_coupling = jax.vmap(lambda own, entries: coupling(own, top_skeleton, entries, inv_scale, scale_amp))(top_skeleton, top_list)
    mid_count = mid_skeleton.shape[0]
    top_count = top_skeleton.shape[0]
    mid_present = mid_list >= 0
    mid_clipped = jnp.where(mid_present, mid_list, 0)
    top_clipped = jnp.where(top_list >= 0, top_list, 0)
    transfer_groups = mid_transfer.reshape(mid_count, -1, R, R)

    def matvec(vector):
        leaf_coef = jnp.einsum('lpn,lrn->lpr', vector.astype(jnp.float32), leaf_basis.astype(jnp.float32))
        leaf_groups = leaf_coef.reshape(mid_count, -1, PROBES, R)
        mid_coef = jnp.einsum('mcpr,mcrs->mps', leaf_groups, transfer_groups, precision=highest)
        top_terms = jnp.einsum('mpr,mrs->mps', mid_coef, top_transfer, precision=highest)
        top_coef = lax.optimization_barrier(jnp.sum(top_terms.reshape(top_count, -1, PROBES, R), axis=1))
        mid_local = jnp.einsum('mkrs,mkps->mpr', mid_coupling, mid_coef[mid_clipped], precision=highest)
        top_local = jnp.einsum('tkrs,tkps->tpr', top_coupling, top_coef[top_clipped], precision=highest)
        top_down = jnp.repeat(top_local, mid_count // top_count, axis=0)
        mid_total = mid_local + jnp.einsum('mps,mrs->mpr', top_down, top_transfer, precision=highest)
        leaf_total = jnp.einsum('mps,mcrs->mcpr', mid_total, transfer_groups, precision=highest)
        leaf_total = leaf_total.reshape(-1, PROBES, R).astype(jnp.bfloat16)
        far = jnp.einsum('lpr,lrn->lpn', leaf_total.astype(jnp.float32), leaf_basis.astype(jnp.float32))
        near = near_part(points, vector, near_list, inv_scale, scale_amp)
        return (noise_var[0] * vector.astype(jnp.float32) + near + far).astype(jnp.bfloat16)
    first_product = matvec(probes)
    second_product = matvec(first_product)
    return (first_product, second_product)
```

```python
import functools
import math

import jax
import jax.numpy as jnp
from jax import lax
from jax.experimental import pallas as pl
from jax.experimental.pallas import tpu as pltpu
from jax.sharding import PartitionSpec as P

MESH = pl.DeviceIdType.MESH
F32 = jnp.float32
BF16 = jnp.bfloat16
LEAFS = 64
MIDS = 8
GROUP = 8
NEAR = 8
MID_NEAR = 6
TOP_NEAR = 6
TOPS = 32
SUBS = 4
R = 64
PROBES = 32
POINTS = 128
CHUNKS = 4
LOG2E = math.log2(math.e)
LN2 = math.log(2.0)
TINY = 1e-30


def nn(a, b):
    return lax.dot_general(a, b, (((1,), (0,)), ((), ())), preferred_element_type=F32)


def nt(a, b):
    return lax.dot_general(a, b, (((1,), (1,)), ((), ())), preferred_element_type=F32)


def split(a):
    high = a.astype(BF16)
    return high, (a - high.astype(F32)).astype(BF16)


def stacked(a):
    return jnp.concatenate(split(a), axis=0)


def wide_product(both, high, low, op):
    rows = both.shape[0] // 2
    result = op(both, high)
    return result[:rows] + result[rows:] + op(both[:rows], low)


def pack(a):
    half = a.shape[0] // 2
    return jnp.concatenate([a[:half], a[half:]], axis=1)


def unpack(a):
    half = a.shape[1] // 2
    return jnp.concatenate([a[:, :half], a[:, half:]], axis=0)


def three(x):
    high = x.astype(BF16).astype(F32)
    rest = x - high
    mid = rest.astype(BF16).astype(F32)
    low = (rest - mid).astype(BF16).astype(F32)
    return high, mid, low


def features(x, left, right):
    width = x.shape[1]
    high, mid, low = three(x)
    norms = jnp.broadcast_to(jnp.sum(x * x, axis=0, keepdims=True), (8, width))
    norm_high, norm_mid, norm_low = three(norms)
    row = lax.broadcasted_iota(jnp.int32, (8, width), 0)
    one = jnp.ones((8, width), F32)
    zero = jnp.zeros((8, width), F32)
    result = []
    if left:
        extra = jnp.where(row < 3, one, zero)
        for place, part in ((3, norm_high), (4, norm_mid), (5, norm_low)):
            extra = jnp.where(row == place, part, extra)
        result.append(jnp.concatenate([high, high, high, mid, mid, low, extra, zero], axis=0))
    if right:
        extra = jnp.where((row >= 3) & (row < 6), one, zero)
        for place, part in ((0, norm_high), (1, norm_mid), (2, norm_low)):
            extra = jnp.where(row == place, part, extra)
        h, m, l = -2.0 * high, -2.0 * mid, -2.0 * low
        result.append(jnp.concatenate([h, m, l, h, m, h, extra, zero], axis=0))
    return result


def matern(squared, amplitude):
    squared = jnp.maximum(squared, TINY)
    u = squared * lax.rsqrt(squared)
    return (amplitude + (amplitude * LN2) * u) * jnp.exp2(-u)


def device_at(position):
    count = TOPS * SUBS
    position = lax.rem(position + count, count)
    return (lax.div(position, SUBS), lax.rem(position, SUBS))


def kernel(
    points_ref,
    probes_ref,
    basis_ref,
    transfer_ref,
    top_transfer_ref,
    mid_skeleton_ref,
    top_skeleton_ref,
    near_list,
    mid_list,
    top_list,
    inv_scale,
    amplitude,
    noise_var,
    first_ref,
    second_ref,
    points_v,
    vector_0,
    vector_1,
    result_v,
    basis,
    transfer_v,
    transfer_h,
    transfer_l,
    top_v,
    top_h,
    top_l,
    skeleton,
    left_v,
    right_v,
    blocks,
    mid_left,
    coupling_h,
    coupling_l,
    top_coupling_h,
    top_coupling_l,
    mids_0,
    mids_1,
    mid_both,
    leaf_total,
    sums_0,
    sums_1,
    tops_0,
    tops_1,
    local_sem,
    out_sem,
    bulk_send,
    bulk_recv,
    side_send,
    side_recv,
    sub_send,
    sub_recv,
    near_send,
    near_recv,
    far_send,
    far_recv,
):
    leaf = lax.axis_index("leaf")
    sub = lax.axis_index("sub")
    position = leaf * SUBS + sub
    plane = lax.div(leaf, 8)
    place = lax.rem(leaf, 8)
    before = device_at(position - 1)
    after = device_at(position + 1)
    sub_ids = [(leaf, lax.rem(sub + k, SUBS)) for k in range(1, SUBS)]
    near_ids = [(plane * 8 + lax.rem(place + k, 8), sub) for k in range(1, 8)]
    far_ids = [(lax.rem(leaf + 8 * k, TOPS), sub) for k in range(1, 4)]

    barrier = pltpu.get_barrier_semaphore()
    partners = [before, after, *sub_ids, *near_ids, *far_ids]
    for partner in partners:
        pl.semaphore_signal(barrier, inc=1, device_id=partner, device_id_type=MESH)

    own = pl.ds(LEAFS, LEAFS)
    loads = [
        pltpu.make_async_copy(source, target, local_sem.at[k])
        for k, (source, target) in enumerate(
            (
                (probes_ref, vector_0.at[own]),
                (basis_ref, basis),
                (transfer_ref, transfer_v),
                (top_transfer_ref, top_v),
                (points_ref, points_v.at[own]),
                (mid_skeleton_ref, skeleton.at[pl.ds(MIDS, MIDS)]),
            )
        )
    ]
    for load in loads:
        load.start()
    pl.semaphore_wait(barrier, len(partners))

    def remote(source, target, send, recv, device):
        return pltpu.make_async_remote_copy(
            src_ref=source,
            dst_ref=target,
            send_sem=send,
            recv_sem=recv,
            device_id=device,
            device_id_type=MESH,
        )

    def halo(source, start, target, first, count, total, send, recv):
        rows = pl.ds(start + first, count)
        return [
            remote(source.at[rows], target.at[pl.ds(first, count)], send.at[0], recv.at[0], after),
            remote(
                source.at[rows],
                target.at[pl.ds(2 * total + first, count)],
                send.at[1],
                recv.at[1],
                before,
            ),
        ]

    per_chunk = LEAFS // CHUNKS
    points_halo = halo(
        points_ref, 0, points_v, 0, LEAFS, LEAFS, side_send.at[0], side_recv.at[0]
    )
    skeleton_halo = halo(
        mid_skeleton_ref, 0, skeleton, 0, MIDS, MIDS, side_send.at[1], side_recv.at[1]
    )
    probes_halo = [
        halo(
            probes_ref,
            0,
            vector_0,
            k * per_chunk,
            per_chunk,
            LEAFS,
            bulk_send.at[0, k],
            bulk_recv.at[0, k],
        )
        for k in range(CHUNKS)
    ]
    for copy in [*points_halo, *skeleton_halo, *probes_halo[0], *probes_halo[1]]:
        copy.start()

    row = lax.broadcasted_iota(jnp.int32, (8, POINTS), 0)
    scales = jnp.zeros((8, POINTS), F32)
    for feature in range(8):
        scales = jnp.where(row == feature, inv_scale[feature] * (math.sqrt(3.0) * LOG2E), scales)

    amp = amplitude[0]
    noise = noise_var[0]

    for load in loads[:4]:
        load.wait()

    def split_transfer(c, carry):
        transfer_h[c], transfer_l[c] = split(transfer_v[c])
        return carry

    lax.fori_loop(0, LEAFS, split_transfer, 0)
    for m in range(MIDS):
        top_h[m], top_l[m] = split(top_v[m])

    def upward(vector, mids, sums):
        def step(m, partial):
            total = jnp.zeros((PROBES, R), F32)
            for c in range(GROUP):
                leaf_id = m * GROUP + c
                coef = nt(vector[LEAFS + leaf_id], basis[leaf_id])
                total += wide_product(stacked(coef), transfer_h[leaf_id], transfer_l[leaf_id], nn)
            mids[MIDS + m] = pack(total)
            both = stacked(total)
            mid_both[MIDS + m] = both
            return partial + wide_product(both, top_h[m], top_l[m], nn)

        partial = lax.fori_loop(0, MIDS, step, jnp.zeros((PROBES, R), F32))
        sums[sub] = pack(partial)

    def small_copies(turn, mids, sums, tops):
        sides = halo(mids, MIDS, mids, 0, MIDS, MIDS, side_send.at[2 + turn], side_recv.at[2 + turn])
        in_sub = [
            remote(sums.at[sub], sums.at[sub], sub_send.at[turn, k], sub_recv.at[turn, k], device)
            for k, device in enumerate(sub_ids)
        ]
        in_plane = [
            remote(
                tops.at[leaf], tops.at[leaf], near_send.at[turn, k], near_recv.at[turn, k], device
            )
            for k, device in enumerate(near_ids)
        ]
        rows = pl.ds(plane * 8, 8)
        over_planes = [
            remote(
                tops.at[rows], tops.at[rows], far_send.at[turn, k], far_recv.at[turn, k], device
            )
            for k, device in enumerate(far_ids)
        ]
        return sides, in_sub, in_plane, over_planes

    def begin(copies):
        for copy in copies:
            copy.start()

    def finish(copies):
        for copy in copies:
            copy.wait()

    def sum_tops(sums, tops):
        total = sums[0]
        for k in range(1, SUBS):
            total += sums[k]
        tops[leaf] = total

    def mid_target(m, e):
        listed = mid_list[m, e]
        target = listed - position * MIDS + MIDS
        return listed, jnp.clip(target, 0, 3 * MIDS - 1)

    def downward(mids, tops):
        def take(m, carry):
            mid_both[m] = stacked(unpack(mids[m]))
            return carry

        lax.fori_loop(0, MIDS, take, 0)
        lax.fori_loop(2 * MIDS, 3 * MIDS, take, 0)
        top_local = jnp.zeros((PROBES, R), F32)
        for e in range(TOP_NEAR):
            target = jnp.clip(top_list[0, e], 0, TOPS - 1)
            top_local += wide_product(
                stacked(unpack(tops[target])), top_coupling_h[e], top_coupling_l[e], nn
            )
        top_both = stacked(top_local)

        def step(m, carry):
            total = wide_product(top_both, top_h[m], top_l[m], nt)
            for e in range(MID_NEAR):
                _, target = mid_target(m, e)
                total += wide_product(mid_both[target], coupling_h[m, e], coupling_l[m, e], nn)
            both = stacked(total)
            for c in range(GROUP):
                leaf_id = m * GROUP + c
                leaf_total[leaf_id] = wide_product(
                    both, transfer_h[leaf_id], transfer_l[leaf_id], nt
                ).astype(BF16)
            return carry

        lax.fori_loop(0, MIDS, step, 0)

    def near_target(i, e):
        listed = near_list[i, e]
        target = listed - position * LEAFS + LEAFS
        return listed, jnp.clip(target, 0, 3 * LEAFS - 1)

    def products(vector, result, offset, first, count):
        def step(i, carry):
            parts = []
            for e in range(NEAR):
                _, target = near_target(i, e)
                parts.append(vector[target])
            total = nn(jnp.concatenate(parts, axis=1), blocks[i])
            total += nn(leaf_total[i], basis[i])
            total += noise * vector[LEAFS + i].astype(F32)
            result[offset + i] = total.astype(BF16)
            return carry

        lax.fori_loop(first, first + count, step, 0, unroll=2)

    sides, in_sub, in_plane, over_planes = small_copies(0, mids_0, sums_0, tops_0)
    upward(vector_0, mids_0, sums_0)
    begin(in_sub)
    begin(sides)
    for k in range(2, CHUNKS):
        begin(probes_halo[k])

    loads[4].wait()

    def own_features(i, carry):
        left, right = features(points_v[LEAFS + i] * scales, True, True)
        left_v[LEAFS + i] = left.T.astype(BF16)
        right_v[i] = right.astype(BF16)
        return carry

    lax.fori_loop(0, LEAFS, own_features, 0, unroll=2)

    small_scales = scales[:, :R]
    (top_right,) = features(top_skeleton_ref[leaf] * small_scales, False, True)
    for e in range(TOP_NEAR):
        target = top_list[0, e]
        (top_left,) = features(
            top_skeleton_ref[jnp.clip(target, 0, TOPS - 1)] * small_scales, True, False
        )
        squared = nn(top_left.T.astype(BF16), top_right.astype(BF16))
        value = matern(squared, jnp.where(target >= 0, amp, 0.0))
        top_coupling_h[e], top_coupling_l[e] = split(value)

    finish(in_sub)
    sum_tops(sums_0, tops_0)
    begin(in_plane)

    finish(points_halo)

    def halo_features(i, carry):
        (left,) = features(points_v[i] * scales, True, False)
        left_v[i] = left.T.astype(BF16)
        return carry

    lax.fori_loop(0, LEAFS, halo_features, 0, unroll=2)
    lax.fori_loop(2 * LEAFS, 3 * LEAFS, halo_features, 0, unroll=2)
    finish(in_plane)
    begin(over_planes)

    def near_blocks(i, carry):
        right = right_v[i]
        for e in range(NEAR):
            listed, target = near_target(i, e)
            value = matern(nn(left_v[target], right), jnp.where(listed >= 0, amp, 0.0))
            blocks[i, pl.ds(e * POINTS, POINTS)] = value.astype(BF16)
        return carry

    lax.fori_loop(0, LEAFS, near_blocks, 0)

    loads[5].wait()
    finish(skeleton_halo)

    def mid_features(m, carry):
        (left,) = features(skeleton[m] * small_scales, True, False)
        mid_left[m] = left.T.astype(BF16)
        return carry

    lax.fori_loop(0, 3 * MIDS, mid_features, 0)

    def mid_couplings(m, carry):
        (right,) = features(skeleton[MIDS + m] * small_scales, False, True)
        right = right.astype(BF16)
        for e in range(MID_NEAR):
            listed, target = mid_target(m, e)
            value = matern(nn(mid_left[target], right), jnp.where(listed >= 0, amp, 0.0))
            coupling_h[m, e], coupling_l[m, e] = split(value)
        return carry

    lax.fori_loop(0, MIDS, mid_couplings, 0)

    finish(over_planes)
    finish(sides)
    downward(mids_0, tops_0)
    for chunk in probes_halo:
        finish(chunk)

    first_halo = [
        halo(
            vector_1,
            LEAFS,
            vector_1,
            k * per_chunk,
            per_chunk,
            LEAFS,
            bulk_send.at[1, k],
            bulk_recv.at[1, k],
        )
        for k in range(CHUNKS)
    ]
    sides, in_sub, in_plane, over_planes = small_copies(1, mids_1, sums_1, tops_1)
    for k in range(CHUNKS):
        products(vector_0, vector_1, LEAFS, k * per_chunk, per_chunk)
        if k < CHUNKS // 2:
            begin(first_halo[k])
    upward(vector_1, mids_1, sums_1)
    begin(in_sub)
    begin(sides)
    for k in range(CHUNKS // 2, CHUNKS):
        begin(first_halo[k])
    first_out = pltpu.make_async_copy(vector_1.at[own], first_ref, out_sem.at[CHUNKS])
    first_out.start()

    finish(in_sub)
    sum_tops(sums_1, tops_1)
    begin(in_plane)
    finish(in_plane)
    begin(over_planes)
    finish(over_planes)
    finish(sides)
    downward(mids_1, tops_1)
    for chunk in first_halo:
        finish(chunk)
    outs = []
    for k in range(CHUNKS):
        rows = pl.ds(k * per_chunk, per_chunk)
        products(vector_1, result_v, 0, k * per_chunk, per_chunk)
        out = pltpu.make_async_copy(result_v.at[rows], second_ref.at[rows], out_sem.at[k])
        out.start()
        outs.append(out)
    for out in outs:
        out.wait()
    first_out.wait()


def on_device(*arguments):
    hbm = pl.BlockSpec(memory_space=pl.ANY)
    smem = pl.BlockSpec(memory_space=pltpu.SMEM)
    vmem = pl.BlockSpec(memory_space=pltpu.VMEM)
    dma = pltpu.SemaphoreType.DMA
    wide = (3 * LEAFS, PROBES, POINTS)
    result = jax.ShapeDtypeStruct((LEAFS, PROBES, POINTS), BF16)
    return pl.pallas_call(
        kernel,
        out_shape=(result, result),
        in_specs=[hbm] * 6 + [vmem] + [smem] * 6,
        out_specs=(hbm, hbm),
        scratch_shapes=[
            pltpu.VMEM((3 * LEAFS, 8, POINTS), F32),
            pltpu.VMEM(wide, BF16),
            pltpu.VMEM(wide, BF16),
            pltpu.VMEM((LEAFS, PROBES, POINTS), BF16),
            pltpu.VMEM((LEAFS, R, POINTS), BF16),
            pltpu.VMEM((LEAFS, R, R), F32),
            pltpu.VMEM((LEAFS, R, R), BF16),
            pltpu.VMEM((LEAFS, R, R), BF16),
            pltpu.VMEM((MIDS, R, R), F32),
            pltpu.VMEM((MIDS, R, R), BF16),
            pltpu.VMEM((MIDS, R, R), BF16),
            pltpu.VMEM((3 * MIDS, 8, R), F32),
            pltpu.VMEM((3 * LEAFS, POINTS, R), BF16),
            pltpu.VMEM((LEAFS, R, POINTS), BF16),
            pltpu.VMEM((LEAFS, NEAR * POINTS, POINTS), BF16),
            pltpu.VMEM((3 * MIDS, R, R), BF16),
            pltpu.VMEM((MIDS, MID_NEAR, R, R), BF16),
            pltpu.VMEM((MIDS, MID_NEAR, R, R), BF16),
            pltpu.VMEM((TOP_NEAR, R, R), BF16),
            pltpu.VMEM((TOP_NEAR, R, R), BF16),
            pltpu.VMEM((3 * MIDS, PROBES // 2, 2 * R), F32),
            pltpu.VMEM((3 * MIDS, PROBES // 2, 2 * R), F32),
            pltpu.VMEM((3 * MIDS, 2 * PROBES, R), BF16),
            pltpu.VMEM((LEAFS, PROBES, R), BF16),
            pltpu.VMEM((SUBS, PROBES // 2, 2 * R), F32),
            pltpu.VMEM((SUBS, PROBES // 2, 2 * R), F32),
            pltpu.VMEM((TOPS, PROBES // 2, 2 * R), F32),
            pltpu.VMEM((TOPS, PROBES // 2, 2 * R), F32),
            dma((6,)),
            dma((CHUNKS + 1,)),
            dma((2, CHUNKS, 2)),
            dma((2, CHUNKS, 2)),
            dma((4, 2)),
            dma((4, 2)),
            dma((2, 3)),
            dma((2, 3)),
            dma((2, 7)),
            dma((2, 7)),
            dma((2, 3)),
            dma((2, 3)),
        ],
        compiler_params=pltpu.CompilerParams(
            collective_id=0, has_side_effects=True, vmem_limit_bytes=56 << 20
        ),
        cost_estimate=pl.CostEstimate(
            flops=6_000_000_000, bytes_accessed=6_000_000, transcendentals=17_000_000
        ),
    )(*arguments)


def solution(mesh):
    split_over_both = P(("leaf", "sub"), None, None)
    in_specs = (
        split_over_both,
        split_over_both,
        split_over_both,
        split_over_both,
        split_over_both,
        split_over_both,
        P(),
        P(("leaf", "sub"), None),
        P(("leaf", "sub"), None),
        P("leaf", None),
        P(),
        P(),
        P(),
    )
    return jax.shard_map(
        on_device,
        mesh=mesh,
        in_specs=in_specs,
        out_specs=(split_over_both, split_over_both),
        check_vma=False,
    )
```

```python
import functools
import math

import jax
import jax.numpy as jnp
from jax import lax
from jax.experimental import pallas as pl
from jax.experimental.pallas import tpu as pltpu
from jax.sharding import PartitionSpec as P

MESH = pl.DeviceIdType.MESH
F32 = jnp.float32
BF16 = jnp.bfloat16
LEAFS = 64
MIDS = 8
GROUP = 8
NEAR = 8
MID_NEAR = 6
TOP_NEAR = 6
TOPS = 32
SUBS = 4
R = 64
PROBES = 32
POINTS = 128
CHUNKS = 4
LOG2E = math.log2(math.e)
LN2 = math.log(2.0)
TINY = 1e-30


def nn(a, b):
    return lax.dot_general(a, b, (((1,), (0,)), ((), ())), preferred_element_type=F32)


def nt(a, b):
    return lax.dot_general(a, b, (((1,), (1,)), ((), ())), preferred_element_type=F32)


def split(a):
    high = a.astype(BF16)
    return high, (a - high.astype(F32)).astype(BF16)


def stacked(a):
    return jnp.concatenate(split(a), axis=0)


def wide_product(both, high, low, op):
    rows = both.shape[0] // 2
    result = op(both, high)
    return result[:rows] + result[rows:] + op(both[:rows], low)


def pack(a):
    half = a.shape[0] // 2
    return jnp.concatenate([a[:half], a[half:]], axis=1)


def unpack(a):
    half = a.shape[1] // 2
    return jnp.concatenate([a[:, :half], a[:, half:]], axis=0)


def three(x):
    high = x.astype(BF16).astype(F32)
    rest = x - high
    mid = rest.astype(BF16).astype(F32)
    low = (rest - mid).astype(BF16).astype(F32)
    return high, mid, low


def features(x, left, right):
    width = x.shape[1]
    high, mid, low = three(x)
    norms = jnp.broadcast_to(jnp.sum(x * x, axis=0, keepdims=True), (8, width))
    norm_high, norm_mid, norm_low = three(norms)
    row = lax.broadcasted_iota(jnp.int32, (8, width), 0)
    one = jnp.ones((8, width), F32)
    zero = jnp.zeros((8, width), F32)
    result = []
    if left:
        extra = jnp.where(row < 3, one, zero)
        for place, part in ((3, norm_high), (4, norm_mid), (5, norm_low)):
            extra = jnp.where(row == place, part, extra)
        result.append(jnp.concatenate([high, high, high, mid, mid, low, extra, zero], axis=0))
    if right:
        extra = jnp.where((row >= 3) & (row < 6), one, zero)
        for place, part in ((0, norm_high), (1, norm_mid), (2, norm_low)):
            extra = jnp.where(row == place, part, extra)
        h, m, l = -2.0 * high, -2.0 * mid, -2.0 * low
        result.append(jnp.concatenate([h, m, l, h, m, h, extra, zero], axis=0))
    return result


def matern(squared, amplitude):
    squared = jnp.maximum(squared, TINY)
    u = squared * lax.rsqrt(squared)
    return (amplitude + (amplitude * LN2) * u) * jnp.exp2(-u)


def device_at(position):
    count = TOPS * SUBS
    position = lax.rem(position + count, count)
    return (lax.div(position, SUBS), lax.rem(position, SUBS))


def kernel(
    points_ref,
    probes_ref,
    basis_ref,
    transfer_ref,
    top_transfer_ref,
    mid_skeleton_ref,
    top_skeleton_ref,
    near_list_ref,
    mid_list,
    top_list,
    inv_scale,
    amplitude,
    noise_var,
    first_ref,
    second_ref,
    points_v,
    vector_0,
    vector_1,
    result_v,
    basis,
    transfer_v,
    transfer_h,
    transfer_l,
    top_v,
    top_h,
    top_l,
    skeleton,
    left_v,
    right_v,
    blocks,
    distance_v,
    mid_left,
    mid_coupling,
    top_coupling,
    mids_0,
    mids_1,
    mid_total,
    part,
    sums_0,
    sums_1,
    tops_0,
    tops_1,
    near_list,
    local_sem,
    out_sem,
    bulk_send,
    bulk_recv,
    side_send,
    side_recv,
    sub_send,
    sub_recv,
    top_send,
    top_recv,
):
    leaf = lax.axis_index("leaf")
    sub = lax.axis_index("sub")
    position = leaf * SUBS + sub
    before = device_at(position - 1)
    after = device_at(position + 1)
    sub_ids = [(leaf, lax.rem(sub + k, SUBS)) for k in range(1, SUBS)]
    top_ids = [(lax.rem(leaf + k, TOPS), sub) for k in range(1, TOPS)]

    barrier = pltpu.get_barrier_semaphore()
    partners = [before, after, *sub_ids, *top_ids]
    for partner in partners:
        pl.semaphore_signal(barrier, inc=1, device_id=partner, device_id_type=MESH)

    own = pl.ds(LEAFS, LEAFS)
    loads = [
        pltpu.make_async_copy(source, target, local_sem.at[k])
        for k, (source, target) in enumerate(
            (
                (probes_ref, vector_0.at[own]),
                (basis_ref, basis),
                (transfer_ref, transfer_v),
                (top_transfer_ref, top_v),
                (points_ref, points_v.at[own]),
                (mid_skeleton_ref, skeleton.at[pl.ds(MIDS, MIDS)]),
                (near_list_ref, near_list),
            )
        )
    ]
    for load in loads:
        load.start()
    pl.semaphore_wait(barrier, len(partners))

    def remote(source, target, send, recv, device):
        return pltpu.make_async_remote_copy(
            src_ref=source,
            dst_ref=target,
            send_sem=send,
            recv_sem=recv,
            device_id=device,
            device_id_type=MESH,
        )

    def halo(source, start, target, first, count, total, send, recv):
        rows = pl.ds(start + first, count)
        return [
            remote(source.at[rows], target.at[pl.ds(first, count)], send.at[0], recv.at[0], after),
            remote(
                source.at[rows],
                target.at[pl.ds(2 * total + first, count)],
                send.at[1],
                recv.at[1],
                before,
            ),
        ]

    per_chunk = LEAFS // CHUNKS
    points_halo = halo(
        points_ref, 0, points_v, 0, LEAFS, LEAFS, side_send.at[0], side_recv.at[0]
    )
    skeleton_halo = halo(
        mid_skeleton_ref, 0, skeleton, 0, MIDS, MIDS, side_send.at[1], side_recv.at[1]
    )
    probes_halo = [
        halo(
            probes_ref,
            0,
            vector_0,
            k * per_chunk,
            per_chunk,
            LEAFS,
            bulk_send.at[0, k],
            bulk_recv.at[0, k],
        )
        for k in range(CHUNKS)
    ]
    for copy in [*points_halo, *skeleton_halo, *probes_halo[0], *probes_halo[1]]:
        copy.start()

    row = lax.broadcasted_iota(jnp.int32, (8, POINTS), 0)
    scales = jnp.zeros((8, POINTS), F32)
    for feature in range(8):
        scales = jnp.where(row == feature, inv_scale[feature] * (math.sqrt(3.0) * LOG2E), scales)

    amp = amplitude[0]
    noise = noise_var[0]

    for load in loads[:4]:
        load.wait()

    def split_transfer(c, carry):
        transfer_h[c], transfer_l[c] = split(transfer_v[c])
        return carry

    lax.fori_loop(0, LEAFS, split_transfer, 0)
    for m in range(MIDS):
        top_h[m], top_l[m] = split(top_v[m])

    lane = lax.broadcasted_iota(jnp.int32, (PROBES, 2 * R), 1)
    lower = lane < R

    def upward(vector, mids, sums):
        def step(m, partial):
            parts = []
            for c in range(0, GROUP, 2):
                leaf_id = m * GROUP + c
                pair = vector[pl.ds(LEAFS + leaf_id, 2)].reshape(2 * PROBES, POINTS)
                coef = nt(pair, basis[pl.ds(leaf_id, 2)].reshape(2 * R, POINTS))
                parts.append(jnp.where(lower, coef[:PROBES], coef[PROBES:]))
            total = wide_product(
                stacked(jnp.concatenate(parts, axis=1)),
                transfer_h[pl.ds(m * GROUP, GROUP)].reshape(GROUP * R, R),
                transfer_l[pl.ds(m * GROUP, GROUP)].reshape(GROUP * R, R),
                nn,
            )
            mids[MIDS + m] = jnp.concatenate([total, total], axis=1).astype(BF16)
            return partial + wide_product(stacked(total), top_h[m], top_l[m], nn)

        sums[sub] = pack(lax.fori_loop(0, MIDS, step, jnp.zeros((PROBES, R), F32), unroll=2))

    def small_copies(turn, mids, sums, tops):
        sides = halo(mids, MIDS, mids, 0, MIDS, MIDS, side_send.at[2 + turn], side_recv.at[2 + turn])
        in_sub = [
            remote(sums.at[sub], sums.at[sub], sub_send.at[turn, k], sub_recv.at[turn, k], device)
            for k, device in enumerate(sub_ids)
        ]
        over_tops = [
            remote(tops.at[leaf], tops.at[leaf], top_send.at[turn, k], top_recv.at[turn, k], device)
            for k, device in enumerate(top_ids)
        ]
        return sides, in_sub, over_tops

    def begin(copies):
        for copy in copies:
            copy.start()

    def finish(copies):
        for copy in copies:
            copy.wait()

    def sum_tops(sums, tops):
        total = sums[0]
        for k in range(1, SUBS):
            total += sums[k]
        tops[leaf] = total.astype(BF16)

    def mid_target(m, e):
        listed = mid_list[m, e]
        target = listed - position * MIDS + MIDS
        return listed, jnp.clip(target, 0, 3 * MIDS - 1)

    def downward(mids, tops, use):
        parts = []
        for e in range(TOP_NEAR):
            both = unpack(tops[jnp.clip(top_list[0, e], 0, TOPS - 1)].astype(F32))
            parts.append(jnp.concatenate([both, both], axis=1).astype(BF16))
        top_both = stacked(nn(jnp.concatenate(parts, axis=1), top_coupling[...]))

        def total_step(m, carry):
            total = wide_product(top_both, top_h[m], top_l[m], nt)
            near = jnp.concatenate([mids[mid_target(m, e)[1]] for e in range(MID_NEAR)], axis=1)
            mid_total[m] = stacked(total + nn(near, mid_coupling[m]))
            return carry

        lax.fori_loop(0, MIDS, total_step, 0, unroll=4)

        def step(m, carry):
            totals = wide_product(
                mid_total[m],
                transfer_h[pl.ds(m * GROUP, GROUP)].reshape(GROUP * R, R),
                transfer_l[pl.ds(m * GROUP, GROUP)].reshape(GROUP * R, R),
                nt,
            )
            for c in range(0, GROUP, 2):
                leaf_id = m * GROUP + c
                pair = totals[:, c * R : (c + 2) * R]
                pair = jnp.concatenate(
                    [jnp.where(lower, pair, 0.0), jnp.where(lower, 0.0, pair)], axis=0
                ).astype(BF16)
                far = nn(pair, basis[pl.ds(leaf_id, 2)].reshape(2 * R, POINTS))
                use(leaf_id, far.reshape(2, PROBES, POINTS))
            return carry

        lax.fori_loop(0, MIDS, step, 0, unroll=2)

    def near_target(i, e):
        listed = near_list[e, i]
        target = listed - position * LEAFS + LEAFS
        return listed, jnp.clip(target, 0, 3 * LEAFS - 1)

    def near_products(vector, first, count, use):
        def step(i, carry):
            parts = [vector[near_target(i, e)[1]] for e in range(NEAR)]
            total = nn(jnp.concatenate(parts, axis=1), blocks[i])
            use(i, total + noise * vector[LEAFS + i].astype(F32))
            return carry

        lax.fori_loop(first, first + count, step, 0, unroll=8)

    sides, in_sub, over_tops = small_copies(0, mids_0, sums_0, tops_0)
    upward(vector_0, mids_0, sums_0)
    begin(in_sub)
    begin(sides)
    for k in range(2, CHUNKS):
        begin(probes_halo[k])

    loads[4].wait()
    loads[6].wait()

    def own_features(i, carry):
        left, right = features(points_v[LEAFS + i] * scales, True, True)
        left_v[LEAFS + i] = left.T.astype(BF16)
        right_v[i] = right.astype(BF16)
        return carry

    lax.fori_loop(0, LEAFS, own_features, 0, unroll=2)

    small_scales = scales[:, :R]
    (top_right,) = features(top_skeleton_ref[leaf] * small_scales, False, True)
    top_right = top_right.astype(BF16)
    for e in range(TOP_NEAR):
        target = top_list[0, e]
        (top_left,) = features(
            top_skeleton_ref[jnp.clip(target, 0, TOPS - 1)] * small_scales, True, False
        )
        value = matern(
            nn(top_left.T.astype(BF16), top_right), jnp.where(target >= 0, amp, 0.0)
        )
        top_coupling[pl.ds(e * POINTS, POINTS)] = stacked(value)

    finish(in_sub)
    sum_tops(sums_0, tops_0)
    begin(over_tops)

    loads[5].wait()
    finish(skeleton_halo)

    def mid_features(m, carry):
        (left,) = features(skeleton[m] * small_scales, True, False)
        mid_left[m] = left.T.astype(BF16)
        return carry

    lax.fori_loop(0, 3 * MIDS, mid_features, 0, unroll=2)

    def mid_couplings(m, carry):
        (right,) = features(skeleton[MIDS + m] * small_scales, False, True)
        right = right.astype(BF16)
        for e in range(MID_NEAR):
            listed, target = mid_target(m, e)
            value = matern(nn(mid_left[target], right), jnp.where(listed >= 0, amp, 0.0))
            mid_coupling[m, pl.ds(e * POINTS, POINTS)] = stacked(value)
        return carry

    lax.fori_loop(0, MIDS, mid_couplings, 0)

    finish(points_halo)

    def halo_features(i, carry):
        (left,) = features(points_v[i] * scales, True, False)
        left_v[i] = left.T.astype(BF16)
        return carry

    lax.fori_loop(0, LEAFS, halo_features, 0, unroll=4)
    lax.fori_loop(2 * LEAFS, 3 * LEAFS, halo_features, 0, unroll=4)

    def distances(i, h, e):
        distance_v[h, e] = nn(left_v[near_target(i, e)[1]], right_v[i])

    for h in range(2):
        for e in range(NEAR):
            distances(h, h, e)

    def near_blocks(k, carry):
        for e in range(NEAR):
            for h in range(2):
                i = 2 * k + h
                scale = jnp.where(near_list[e, i] >= 0, amp, 0.0)
                value = matern(distance_v[h, e], scale)
                blocks[i, pl.ds(e * POINTS, POINTS)] = value.astype(BF16)
                distances(jnp.minimum(i + 2, LEAFS - 1), h, e)
        return carry

    lax.fori_loop(0, LEAFS // 2, near_blocks, 0)

    finish(over_tops)
    finish(sides)

    def keep_far(i, far):
        part[pl.ds(i, 2)] = far

    downward(mids_0, tops_0, keep_far)
    for chunk in probes_halo:
        finish(chunk)

    first_halo = [
        halo(
            vector_1,
            LEAFS,
            vector_1,
            k * per_chunk,
            per_chunk,
            LEAFS,
            bulk_send.at[1, k],
            bulk_recv.at[1, k],
        )
        for k in range(CHUNKS)
    ]

    def finish_first(i, near):
        vector_1[LEAFS + i] = (near + part[i]).astype(BF16)

    for k in range(CHUNKS):
        near_products(vector_0, k * per_chunk, per_chunk, finish_first)
        if k < CHUNKS - 1:
            begin(first_halo[k])
    sides, in_sub, over_tops = small_copies(1, mids_1, sums_1, tops_1)
    upward(vector_1, mids_1, sums_1)
    begin(in_sub)
    begin(sides)
    begin(first_halo[CHUNKS - 1])
    first_out = pltpu.make_async_copy(vector_1.at[own], first_ref, out_sem.at[CHUNKS])
    first_out.start()

    finish(in_sub)
    sum_tops(sums_1, tops_1)
    begin(over_tops)
    for chunk in first_halo:
        finish(chunk)

    def keep_near(i, near):
        part[i] = near

    near_products(vector_1, 0, LEAFS, keep_near)
    finish(over_tops)
    finish(sides)

    def finish_second(i, far):
        result_v[pl.ds(i, 2)] = (far + part[pl.ds(i, 2)]).astype(BF16)

    downward(mids_1, tops_1, finish_second)
    second_out = pltpu.make_async_copy(result_v, second_ref, out_sem.at[0])
    second_out.start()
    second_out.wait()
    first_out.wait()


def copy_out(first_ref, second_ref, first_out, second_out, held, in_sem, out_sem):
    rows = LEAFS // CHUNKS
    into, out = [], []
    for p, (source, target) in enumerate(((first_ref, first_out), (second_ref, second_out))):
        for k in range(CHUNKS):
            some = pl.ds(k * rows, rows)
            into.append(
                pltpu.make_async_copy(source.at[some], held.at[p, some], in_sem.at[p, k])
            )
            out.append(pltpu.make_async_copy(held.at[p, some], target.at[some], out_sem.at[p, k]))
    for copy in into:
        copy.start()
    for k, copy in enumerate(out):
        into[k].wait()
        copy.start()
    for copy in out:
        copy.wait()


def on_device(*arguments):
    hbm = pl.BlockSpec(memory_space=pl.ANY)
    smem = pl.BlockSpec(memory_space=pltpu.SMEM)
    vmem = pl.BlockSpec(memory_space=pltpu.VMEM)
    dma = pltpu.SemaphoreType.DMA
    wide = (3 * LEAFS, PROBES, POINTS)
    result = jax.ShapeDtypeStruct((LEAFS, PROBES, POINTS), BF16)
    products = pl.pallas_call(
        kernel,
        out_shape=(result, result),
        in_specs=[hbm] * 6 + [vmem, hbm] + [smem] * 5,
        out_specs=(hbm, hbm),
        scratch_shapes=[
            pltpu.VMEM((3 * LEAFS, 8, POINTS), F32),
            pltpu.VMEM(wide, BF16),
            pltpu.VMEM(wide, BF16),
            pltpu.VMEM((LEAFS, PROBES, POINTS), BF16),
            pltpu.VMEM((LEAFS, R, POINTS), BF16),
            pltpu.VMEM((LEAFS, R, R), F32),
            pltpu.VMEM((LEAFS, R, R), BF16),
            pltpu.VMEM((LEAFS, R, R), BF16),
            pltpu.VMEM((MIDS, R, R), F32),
            pltpu.VMEM((MIDS, R, R), BF16),
            pltpu.VMEM((MIDS, R, R), BF16),
            pltpu.VMEM((3 * MIDS, 8, R), F32),
            pltpu.VMEM((3 * LEAFS, POINTS, R), BF16),
            pltpu.VMEM((LEAFS, R, POINTS), BF16),
            pltpu.VMEM((LEAFS, NEAR * POINTS, POINTS), BF16),
            pltpu.VMEM((2, NEAR, POINTS, POINTS), F32),
            pltpu.VMEM((3 * MIDS, R, R), BF16),
            pltpu.VMEM((MIDS, MID_NEAR * 2 * R, R), BF16),
            pltpu.VMEM((TOP_NEAR * 2 * R, R), BF16),
            pltpu.VMEM((3 * MIDS, PROBES, 2 * R), BF16),
            pltpu.VMEM((3 * MIDS, PROBES, 2 * R), BF16),
            pltpu.VMEM((MIDS, 2 * PROBES, R), BF16),
            pltpu.VMEM((LEAFS, PROBES, POINTS), F32),
            pltpu.VMEM((SUBS, PROBES // 2, 2 * R), F32),
            pltpu.VMEM((SUBS, PROBES // 2, 2 * R), F32),
            pltpu.VMEM((TOPS, PROBES // 2, 2 * R), BF16),
            pltpu.VMEM((TOPS, PROBES // 2, 2 * R), BF16),
            pltpu.SMEM((NEAR, LEAFS), jnp.int32),
            dma((7,)),
            dma((CHUNKS + 1,)),
            dma((2, CHUNKS, 2)),
            dma((2, CHUNKS, 2)),
            dma((4, 2)),
            dma((4, 2)),
            dma((2, 3)),
            dma((2, 3)),
            dma((2, TOPS - 1)),
            dma((2, TOPS - 1)),
        ],
        compiler_params=pltpu.CompilerParams(
            collective_id=0, has_side_effects=True, vmem_limit_bytes=56 << 20
        ),
        cost_estimate=pl.CostEstimate(
            flops=6_000_000_000, bytes_accessed=6_000_000, transcendentals=17_000_000
        ),
    )(*arguments[:7], arguments[7].T, *arguments[8:])
    return pl.pallas_call(
        copy_out,
        out_shape=(result, result),
        in_specs=[hbm, hbm],
        out_specs=(hbm, hbm),
        scratch_shapes=[
            pltpu.VMEM((2, LEAFS, PROBES, POINTS), BF16),
            dma((2, CHUNKS)),
            dma((2, CHUNKS)),
        ],
    )(*products)


def solution(mesh):
    split_over_both = P(("leaf", "sub"), None, None)
    in_specs = (
        split_over_both,
        split_over_both,
        split_over_both,
        split_over_both,
        split_over_both,
        split_over_both,
        P(),
        P(("leaf", "sub"), None),
        P(("leaf", "sub"), None),
        P("leaf", None),
        P(),
        P(),
        P(),
    )
    return jax.shard_map(
        on_device,
        mesh=mesh,
        in_specs=in_specs,
        out_specs=(split_over_both, split_over_both),
        check_vma=False,
    )
```

```python
import functools
import math

import jax
import jax.numpy as jnp
from jax import lax
from jax.experimental import pallas as pl
from jax.experimental.pallas import tpu as pltpu
from jax.sharding import PartitionSpec as P

MESH = pl.DeviceIdType.MESH
F32 = jnp.float32
BF16 = jnp.bfloat16
LEAFS = 64
MIDS = 8
GROUP = 8
NEAR = 8
MID_NEAR = 6
TOP_NEAR = 6
TOPS = 32
SUBS = 4
R = 64
PROBES = 32
POINTS = 128
CHUNKS = 4
LOG2E = math.log2(math.e)
LN2 = math.log(2.0)
TINY = 1e-30


def nn(a, b):
    return lax.dot_general(a, b, (((1,), (0,)), ((), ())), preferred_element_type=F32)


def nt(a, b):
    return lax.dot_general(a, b, (((1,), (1,)), ((), ())), preferred_element_type=F32)


def split(a):
    high = a.astype(BF16)
    return high, (a - high.astype(F32)).astype(BF16)


def stacked(a):
    return jnp.concatenate(split(a), axis=0)


def wide_product(both, high, low, op):
    rows = both.shape[0] // 2
    result = op(both, high)
    return result[:rows] + result[rows:] + op(both[:rows], low)


def pack(a):
    half = a.shape[0] // 2
    return jnp.concatenate([a[:half], a[half:]], axis=1)


def unpack(a):
    half = a.shape[1] // 2
    return jnp.concatenate([a[:, :half], a[:, half:]], axis=0)


def three(x):
    high = x.astype(BF16).astype(F32)
    rest = x - high
    mid = rest.astype(BF16).astype(F32)
    low = (rest - mid).astype(BF16).astype(F32)
    return high, mid, low


def features(x, left, right):
    width = x.shape[1]
    high, mid, low = three(x)
    norms = jnp.broadcast_to(jnp.sum(x * x, axis=0, keepdims=True), (8, width))
    norm_high, norm_mid, norm_low = three(norms)
    row = lax.broadcasted_iota(jnp.int32, (8, width), 0)
    one = jnp.ones((8, width), F32)
    zero = jnp.zeros((8, width), F32)
    result = []
    if left:
        extra = jnp.where(row < 3, one, zero)
        for place, part in ((3, norm_high), (4, norm_mid), (5, norm_low)):
            extra = jnp.where(row == place, part, extra)
        result.append(jnp.concatenate([high, high, high, mid, mid, low, extra, zero], axis=0))
    if right:
        extra = jnp.where((row >= 3) & (row < 6), one, zero)
        for place, part in ((0, norm_high), (1, norm_mid), (2, norm_low)):
            extra = jnp.where(row == place, part, extra)
        h, m, l = -2.0 * high, -2.0 * mid, -2.0 * low
        result.append(jnp.concatenate([h, m, l, h, m, h, extra, zero], axis=0))
    return result


def matern(squared, amplitude):
    squared = jnp.maximum(squared, TINY)
    u = squared * lax.rsqrt(squared)
    return (amplitude + (amplitude * LN2) * u) * jnp.exp2(-u)


def device_at(position):
    count = TOPS * SUBS
    position = lax.rem(position + count, count)
    return (lax.div(position, SUBS), lax.rem(position, SUBS))


def kernel(
    points_ref,
    probes_ref,
    basis_ref,
    transfer_ref,
    top_transfer_ref,
    mid_skeleton_ref,
    top_skeleton_ref,
    near_list_ref,
    mid_list,
    top_list,
    inv_scale,
    amplitude,
    noise_var,
    first_ref,
    second_ref,
    points_v,
    vector_0,
    vector_1,
    result_v,
    basis,
    transfer_v,
    transfer_h,
    transfer_l,
    top_v,
    top_h,
    top_l,
    skeleton,
    left_v,
    right_v,
    blocks,
    distance_v,
    mid_left,
    mid_coupling,
    top_coupling,
    mids_0,
    mids_1,
    mid_total,
    part,
    sums_0,
    sums_1,
    tops_0,
    tops_1,
    near_list,
    local_sem,
    out_sem,
    bulk_send,
    bulk_recv,
    side_send,
    side_recv,
    sub_send,
    sub_recv,
    top_send,
    top_recv,
):
    leaf = lax.axis_index("leaf")
    sub = lax.axis_index("sub")
    position = leaf * SUBS + sub
    before = device_at(position - 1)
    after = device_at(position + 1)
    sub_ids = [(leaf, lax.rem(sub + k, SUBS)) for k in range(1, SUBS)]
    top_ids = [(lax.rem(leaf + k, TOPS), sub) for k in range(1, TOPS)]

    barrier = pltpu.get_barrier_semaphore()
    partners = [before, after, *sub_ids, *top_ids]
    for partner in partners:
        pl.semaphore_signal(barrier, inc=1, device_id=partner, device_id_type=MESH)

    own = pl.ds(LEAFS, LEAFS)
    loads = [
        pltpu.make_async_copy(source, target, local_sem.at[k])
        for k, (source, target) in enumerate(
            (
                (probes_ref, vector_0.at[own]),
                (basis_ref, basis),
                (transfer_ref, transfer_v),
                (top_transfer_ref, top_v),
                (points_ref, points_v.at[own]),
                (mid_skeleton_ref, skeleton.at[pl.ds(MIDS, MIDS)]),
                (near_list_ref, near_list),
            )
        )
    ]
    for load in loads:
        load.start()
    pl.semaphore_wait(barrier, len(partners))

    def remote(source, target, send, recv, device):
        return pltpu.make_async_remote_copy(
            src_ref=source,
            dst_ref=target,
            send_sem=send,
            recv_sem=recv,
            device_id=device,
            device_id_type=MESH,
        )

    def halo(source, start, target, first, count, total, send, recv):
        rows = pl.ds(start + first, count)
        return [
            remote(source.at[rows], target.at[pl.ds(first, count)], send.at[0], recv.at[0], after),
            remote(
                source.at[rows],
                target.at[pl.ds(2 * total + first, count)],
                send.at[1],
                recv.at[1],
                before,
            ),
        ]

    per_chunk = LEAFS // CHUNKS
    points_halo = halo(
        points_ref, 0, points_v, 0, LEAFS, LEAFS, side_send.at[0], side_recv.at[0]
    )
    skeleton_halo = halo(
        mid_skeleton_ref, 0, skeleton, 0, MIDS, MIDS, side_send.at[1], side_recv.at[1]
    )
    probes_halo = [
        halo(
            probes_ref,
            0,
            vector_0,
            k * per_chunk,
            per_chunk,
            LEAFS,
            bulk_send.at[0, k],
            bulk_recv.at[0, k],
        )
        for k in range(CHUNKS)
    ]
    for copy in [*points_halo, *skeleton_halo]:
        copy.start()

    row = lax.broadcasted_iota(jnp.int32, (8, POINTS), 0)
    scales = jnp.zeros((8, POINTS), F32)
    for feature in range(8):
        scales = jnp.where(row == feature, inv_scale[feature] * (math.sqrt(3.0) * LOG2E), scales)

    amp = amplitude[0]
    noise = noise_var[0]

    for load in loads[:4]:
        load.wait()

    def split_transfer(c, carry):
        transfer_h[c], transfer_l[c] = split(transfer_v[c])
        return carry

    lax.fori_loop(0, LEAFS, split_transfer, 0)
    for m in range(MIDS):
        top_h[m], top_l[m] = split(top_v[m])

    lane = lax.broadcasted_iota(jnp.int32, (PROBES, 2 * R), 1)
    lower = lane < R

    def upward(vector, mids, sums):
        def step(m, partial):
            parts = []
            for c in range(0, GROUP, 2):
                leaf_id = m * GROUP + c
                pair = vector[pl.ds(LEAFS + leaf_id, 2)].reshape(2 * PROBES, POINTS)
                coef = nt(pair, basis[pl.ds(leaf_id, 2)].reshape(2 * R, POINTS))
                parts.append(jnp.where(lower, coef[:PROBES], coef[PROBES:]))
            total = wide_product(
                stacked(jnp.concatenate(parts, axis=1)),
                transfer_h[pl.ds(m * GROUP, GROUP)].reshape(GROUP * R, R),
                transfer_l[pl.ds(m * GROUP, GROUP)].reshape(GROUP * R, R),
                nn,
            )
            mids[MIDS + m] = jnp.concatenate([total, total], axis=1).astype(BF16)
            return partial + wide_product(stacked(total), top_h[m], top_l[m], nn)

        sums[sub] = pack(lax.fori_loop(0, MIDS, step, jnp.zeros((PROBES, R), F32), unroll=2))

    def small_copies(turn, mids, sums, tops):
        sides = halo(mids, MIDS, mids, 0, MIDS, MIDS, side_send.at[2 + turn], side_recv.at[2 + turn])
        in_sub = [
            remote(sums.at[sub], sums.at[sub], sub_send.at[turn, k], sub_recv.at[turn, k], device)
            for k, device in enumerate(sub_ids)
        ]
        over_tops = [
            remote(tops.at[leaf], tops.at[leaf], top_send.at[turn, k], top_recv.at[turn, k], device)
            for k, device in enumerate(top_ids)
        ]
        return sides, in_sub, over_tops

    def begin(copies):
        for copy in copies:
            copy.start()

    def finish(copies):
        for copy in copies:
            copy.wait()

    def sum_tops(sums, tops):
        total = sums[0]
        for k in range(1, SUBS):
            total += sums[k]
        tops[leaf] = total.astype(BF16)

    def mid_target(m, e):
        listed = mid_list[m, e]
        target = listed - position * MIDS + MIDS
        return listed, jnp.clip(target, 0, 3 * MIDS - 1)

    def downward(mids, tops, use):
        parts = []
        for e in range(TOP_NEAR):
            both = unpack(tops[jnp.clip(top_list[0, e], 0, TOPS - 1)].astype(F32))
            parts.append(jnp.concatenate([both, both], axis=1).astype(BF16))
        top_both = stacked(nn(jnp.concatenate(parts, axis=1), top_coupling[...]))

        def total_step(m, carry):
            total = wide_product(top_both, top_h[m], top_l[m], nt)
            near = jnp.concatenate([mids[mid_target(m, e)[1]] for e in range(MID_NEAR)], axis=1)
            mid_total[m] = stacked(total + nn(near, mid_coupling[m]))
            return carry

        lax.fori_loop(0, MIDS, total_step, 0, unroll=4)

        def step(m, carry):
            totals = wide_product(
                mid_total[m],
                transfer_h[pl.ds(m * GROUP, GROUP)].reshape(GROUP * R, R),
                transfer_l[pl.ds(m * GROUP, GROUP)].reshape(GROUP * R, R),
                nt,
            )
            for c in range(0, GROUP, 2):
                leaf_id = m * GROUP + c
                pair = totals[:, c * R : (c + 2) * R]
                pair = jnp.concatenate(
                    [jnp.where(lower, pair, 0.0), jnp.where(lower, 0.0, pair)], axis=0
                ).astype(BF16)
                far = nn(pair, basis[pl.ds(leaf_id, 2)].reshape(2 * R, POINTS))
                use(leaf_id, far.reshape(2, PROBES, POINTS))
            return carry

        lax.fori_loop(0, MIDS, step, 0, unroll=2)

    def near_target(i, e):
        listed = near_list[e, i]
        target = listed - position * LEAFS + LEAFS
        return listed, jnp.clip(target, 0, 3 * LEAFS - 1)

    def near_products(vector, first, count, use):
        def step(i, carry):
            parts = [vector[near_target(i, e)[1]] for e in range(NEAR)]
            total = nn(jnp.concatenate(parts, axis=1), blocks[i])
            use(i, total + noise * vector[LEAFS + i].astype(F32))
            return carry

        lax.fori_loop(first, first + count, step, 0, unroll=8)

    sides, in_sub, over_tops = small_copies(0, mids_0, sums_0, tops_0)
    upward(vector_0, mids_0, sums_0)
    begin(in_sub)
    begin(sides)

    for chunk in probes_halo:
        begin(chunk)

    loads[4].wait()
    loads[6].wait()

    def own_features(i, carry):
        left, right = features(points_v[LEAFS + i] * scales, True, True)
        left_v[LEAFS + i] = left.T.astype(BF16)
        right_v[i] = right.astype(BF16)
        return carry

    lax.fori_loop(0, LEAFS, own_features, 0, unroll=2)

    small_scales = scales[:, :R]
    (top_right,) = features(top_skeleton_ref[leaf] * small_scales, False, True)
    top_right = top_right.astype(BF16)
    for e in range(TOP_NEAR):
        target = top_list[0, e]
        (top_left,) = features(
            top_skeleton_ref[jnp.clip(target, 0, TOPS - 1)] * small_scales, True, False
        )
        value = matern(
            nn(top_left.T.astype(BF16), top_right), jnp.where(target >= 0, amp, 0.0)
        )
        top_coupling[pl.ds(e * POINTS, POINTS)] = stacked(value)

    finish(points_halo)

    def halo_features(i, carry):
        (left,) = features(points_v[i] * scales, True, False)
        left_v[i] = left.T.astype(BF16)
        return carry

    lax.fori_loop(0, LEAFS, halo_features, 0, unroll=4)
    lax.fori_loop(2 * LEAFS, 3 * LEAFS, halo_features, 0, unroll=4)

    finish(in_sub)
    sum_tops(sums_0, tops_0)
    begin(over_tops)

    def distances(i, h, e):
        distance_v[h, e] = nn(left_v[near_target(i, e)[1]], right_v[i])

    for h in range(2):
        for e in range(NEAR):
            distances(h, h, e)

    def near_blocks(k, carry):
        for e in range(NEAR):
            for h in range(2):
                i = 2 * k + h
                scale = jnp.where(near_list[e, i] >= 0, amp, 0.0)
                value = matern(distance_v[h, e], scale)
                blocks[i, pl.ds(e * POINTS, POINTS)] = value.astype(BF16)
                distances(jnp.minimum(i + 2, LEAFS - 1), h, e)
        return carry

    lax.fori_loop(0, LEAFS // 2, near_blocks, 0)

    loads[5].wait()
    finish(skeleton_halo)

    def mid_features(m, carry):
        (left,) = features(skeleton[m] * small_scales, True, False)
        mid_left[m] = left.T.astype(BF16)
        return carry

    lax.fori_loop(0, 3 * MIDS, mid_features, 0, unroll=2)

    def mid_couplings(m, carry):
        (right,) = features(skeleton[MIDS + m] * small_scales, False, True)
        right = right.astype(BF16)
        for e in range(MID_NEAR):
            listed, target = mid_target(m, e)
            value = matern(nn(mid_left[target], right), jnp.where(listed >= 0, amp, 0.0))
            mid_coupling[m, pl.ds(e * POINTS, POINTS)] = stacked(value)
        return carry

    lax.fori_loop(0, MIDS, mid_couplings, 0)

    finish(over_tops)
    finish(sides)

    def keep_far(i, far):
        part[pl.ds(i, 2)] = far

    downward(mids_0, tops_0, keep_far)
    for chunk in probes_halo:
        finish(chunk)

    first_halo = [
        halo(
            vector_1,
            LEAFS,
            vector_1,
            k * per_chunk,
            per_chunk,
            LEAFS,
            bulk_send.at[1, k],
            bulk_recv.at[1, k],
        )
        for k in range(CHUNKS)
    ]

    def finish_first(i, near):
        vector_1[LEAFS + i] = (near + part[i]).astype(BF16)

    for k in range(CHUNKS):
        near_products(vector_0, k * per_chunk, per_chunk, finish_first)
        begin(first_halo[k])
    sides, in_sub, over_tops = small_copies(1, mids_1, sums_1, tops_1)
    upward(vector_1, mids_1, sums_1)
    begin(in_sub)
    begin(sides)
    first_out = pltpu.make_async_copy(vector_1.at[own], first_ref, out_sem.at[CHUNKS])
    first_out.start()

    finish(in_sub)
    sum_tops(sums_1, tops_1)
    begin(over_tops)
    for chunk in first_halo:
        finish(chunk)

    def keep_near(i, near):
        part[i] = near

    near_products(vector_1, 0, LEAFS, keep_near)
    finish(over_tops)
    finish(sides)

    def finish_second(i, far):
        result_v[pl.ds(i, 2)] = (far + part[pl.ds(i, 2)]).astype(BF16)

    downward(mids_1, tops_1, finish_second)
    second_out = pltpu.make_async_copy(result_v, second_ref, out_sem.at[0])
    second_out.start()
    second_out.wait()
    first_out.wait()


def copy_out(first_ref, second_ref, first_out, second_out, held, in_sem, out_sem):
    rows = LEAFS // CHUNKS
    into, out = [], []
    for p, (source, target) in enumerate(((first_ref, first_out), (second_ref, second_out))):
        for k in range(CHUNKS):
            some = pl.ds(k * rows, rows)
            into.append(
                pltpu.make_async_copy(source.at[some], held.at[p, some], in_sem.at[p, k])
            )
            out.append(pltpu.make_async_copy(held.at[p, some], target.at[some], out_sem.at[p, k]))
    for copy in into:
        copy.start()
    for k, copy in enumerate(out):
        into[k].wait()
        copy.start()
    for copy in out:
        copy.wait()


def on_device(*arguments):
    hbm = pl.BlockSpec(memory_space=pl.ANY)
    smem = pl.BlockSpec(memory_space=pltpu.SMEM)
    vmem = pl.BlockSpec(memory_space=pltpu.VMEM)
    dma = pltpu.SemaphoreType.DMA
    wide = (3 * LEAFS, PROBES, POINTS)
    result = jax.ShapeDtypeStruct((LEAFS, PROBES, POINTS), BF16)
    products = pl.pallas_call(
        kernel,
        out_shape=(result, result),
        in_specs=[hbm] * 6 + [vmem, hbm] + [smem] * 5,
        out_specs=(hbm, hbm),
        scratch_shapes=[
            pltpu.VMEM((3 * LEAFS, 8, POINTS), F32),
            pltpu.VMEM(wide, BF16),
            pltpu.VMEM(wide, BF16),
            pltpu.VMEM((LEAFS, PROBES, POINTS), BF16),
            pltpu.VMEM((LEAFS, R, POINTS), BF16),
            pltpu.VMEM((LEAFS, R, R), F32),
            pltpu.VMEM((LEAFS, R, R), BF16),
            pltpu.VMEM((LEAFS, R, R), BF16),
            pltpu.VMEM((MIDS, R, R), F32),
            pltpu.VMEM((MIDS, R, R), BF16),
            pltpu.VMEM((MIDS, R, R), BF16),
            pltpu.VMEM((3 * MIDS, 8, R), F32),
            pltpu.VMEM((3 * LEAFS, POINTS, R), BF16),
            pltpu.VMEM((LEAFS, R, POINTS), BF16),
            pltpu.VMEM((LEAFS, NEAR * POINTS, POINTS), BF16),
            pltpu.VMEM((2, NEAR, POINTS, POINTS), F32),
            pltpu.VMEM((3 * MIDS, R, R), BF16),
            pltpu.VMEM((MIDS, MID_NEAR * 2 * R, R), BF16),
            pltpu.VMEM((TOP_NEAR * 2 * R, R), BF16),
            pltpu.VMEM((3 * MIDS, PROBES, 2 * R), BF16),
            pltpu.VMEM((3 * MIDS, PROBES, 2 * R), BF16),
            pltpu.VMEM((MIDS, 2 * PROBES, R), BF16),
            pltpu.VMEM((LEAFS, PROBES, POINTS), F32),
            pltpu.VMEM((SUBS, PROBES // 2, 2 * R), F32),
            pltpu.VMEM((SUBS, PROBES // 2, 2 * R), F32),
            pltpu.VMEM((TOPS, PROBES // 2, 2 * R), BF16),
            pltpu.VMEM((TOPS, PROBES // 2, 2 * R), BF16),
            pltpu.SMEM((NEAR, LEAFS), jnp.int32),
            dma((7,)),
            dma((CHUNKS + 1,)),
            dma((2, CHUNKS, 2)),
            dma((2, CHUNKS, 2)),
            dma((4, 2)),
            dma((4, 2)),
            dma((2, 3)),
            dma((2, 3)),
            dma((2, TOPS - 1)),
            dma((2, TOPS - 1)),
        ],
        compiler_params=pltpu.CompilerParams(
            collective_id=0, has_side_effects=True, vmem_limit_bytes=56 << 20
        ),
        cost_estimate=pl.CostEstimate(
            flops=6_000_000_000, bytes_accessed=6_000_000, transcendentals=17_000_000
        ),
    )(*arguments[:7], arguments[7].T, *arguments[8:])
    return pl.pallas_call(
        copy_out,
        out_shape=(result, result),
        in_specs=[hbm, hbm],
        out_specs=(hbm, hbm),
        scratch_shapes=[
            pltpu.VMEM((2, LEAFS, PROBES, POINTS), BF16),
            dma((2, CHUNKS)),
            dma((2, CHUNKS)),
        ],
    )(*products)


def solution(mesh):
    split_over_both = P(("leaf", "sub"), None, None)
    in_specs = (
        split_over_both,
        split_over_both,
        split_over_both,
        split_over_both,
        split_over_both,
        split_over_both,
        P(),
        P(("leaf", "sub"), None),
        P(("leaf", "sub"), None),
        P("leaf", None),
        P(),
        P(),
        P(),
    )
    return jax.shard_map(
        on_device,
        mesh=mesh,
        in_specs=in_specs,
        out_specs=(split_over_both, split_over_both),
        check_vma=False,
    )
```
